32 devices in a mesh: dp: 8 (over z, y), mp: 4 (over x, core).
Axes of the slice: x: 2, y: 2, z: 4, core: 2. Of those that a mesh axis runs over, the one named last changes fastest.
Arguments:
- block_input: bfloat16 [8192, 768], P('dp'), may hold values from -6 to 6
- seq_lengths: int32 [8], P('dp'), may hold values from 1 to 1024, 4096 in all
- first_gain: float32 [768], replicated, may hold values from 0.5 to 1.5
- first_shift: float32 [768], replicated, may hold values from -3 to 3
- qkv_weight: bfloat16 [3, 768, 768], P(None, None, 'mp'), may hold values from -0.3125 to 0.3125
- qv_bias: float32 [2, 768], P(None, 'mp'), may hold values from -3 to 3
- out_weight: bfloat16 [768, 768], P('mp'), may hold values from -6 to 6
- out_bias: float32 [768], replicated, may hold values from -4 to 4
- second_gain: float32 [768], replicated, may hold values from 0.5 to 1.5
- second_shift: float32 [768], replicated, may hold values from -3 to 3
- fc_weight: bfloat16 [768, 3072], P(None, 'mp'), may hold values from -0.21875 to 0.21875
- fc_bias: float32 [3072], P('mp'), may hold values from -3 to 3
- down_weight: bfloat16 [3072, 768], P('mp'), may hold values from -1.25 to 1.25
- down_bias: float32 [768], replicated, may hold values from -4 to 4
- cotangent: bfloat16 [8192, 768], P('dp'), may hold values from -6 to 6
Outputs:
- block_output: bfloat16 [8192, 768], P('dp')
- input_grad: float32 [8192, 768], P('dp')
- first_gain_grad: float32 [768], replicated
- first_shift_grad: float32 [768], replicated
- qkv_grad: float32 [3, 768, 768], P(None, None, 'mp')
- qv_bias_grad: float32 [2, 768], P(None, 'mp')
- out_weight_grad: float32 [768, 768], P('mp')
- out_bias_grad: float32 [768], replicated
- second_gain_grad: float32 [768], replicated
- second_shift_grad: float32 [768], replicated
- fc_weight_grad: float32 [768, 3072], P(None, 'mp')
- fc_bias_grad: float32 [3072], P('mp')
- down_weight_grad: float32 [3072, 768], P('mp')
- down_bias_grad: float32 [768], replicated
The draws below stay inside these ranges and needn't reach their ends.
Inputs may be any that keep to these rules, and one draw needn't show every extreme that they name: `seq_lengths`: each sequence's true length; in every draw at least one sequence fills all 1024 slots.
All inputs are finite; a program needn't handle non-finite values. No bound on the sum of `seq_lengths` on one device may be relied on, other than what follows from the above.
Results may differ from the reference program's by a relative error of at most 0.011.
The reference program's roundings to bfloat16 on the way count: a program that leaves them out, or rounds other values in their place, can miss the bound.
Values sent between devices are 32-bit elements; how exact they have to be, the bound alone decides.
No kernel may reach another device: no remote copies, remote signals or barrier semaphores. Data moves between devices by JAX's collectives and lax.ppermute only.
A program may use at most 128 MiB of HBM per device.

```python
import math
import jax
import jax.numpy as jnp
import numpy as np
from jax import lax

D = 768
HEADS = 12
HD = 64
FF = 3072
LEN = 1024
BATCH = 8
TOKENS = 8192


def block_levels(key, extent, shards, least, high):
    factor_of, own = 1.0, jax.random.fold_in(key, 6)
    for axis_at, blocks in shards:
        draws = jnp.exp(jax.random.uniform(jax.random.fold_in(own, axis_at), (blocks,), jnp.float32, least / len(shards), high / len(shards)))
        factor_of = factor_of * jnp.repeat(draws, extent[axis_at] // blocks).reshape([-1 if axis == axis_at else 1 for axis in range(len(extent))])
    return factor_of


def profile(amount, total, bound, slope):
    loads = [(1 << 20) // math.isqrt(grade ** slope) + 1 for grade in range(2, amount + 1)]
    rest, given = total - bound - (amount - 1), [1] * (amount - 1)
    while rest > 0:
        movable = [i for i in range(amount - 1) if given[i] < bound]
        whole, remaining = sum([loads[i] for i in movable]), rest
        for i in movable:
            more = min(bound - given[i], max(1, remaining * loads[i] // whole), rest)
            given[i] = given[i] + more
            rest = rest - more
    return np.array([bound] + given)


def ragged_sizes(key, amount, total, bound, skew):
    if amount == 2:
        one = jax.random.randint(key, (), max(1, total - bound), min(bound, total - 1) + 1)
        return jnp.stack([one, total - one])
    lengths = jnp.asarray(profile(amount, total, bound, skew), jnp.int32)
    pairs = (amount - 1) // 2
    donor, taker = lengths[1:1 + 2 * pairs:2], lengths[2:2 + 2 * pairs:2]
    room = jnp.minimum(donor - 1, bound - taker)
    passed = jax.random.randint(jax.random.fold_in(key, 1), (pairs,), 0, 1 << 20) % (room + 1)
    lengths = lengths.at[1:1 + 2 * pairs:2].set(donor - passed).at[2:2 + 2 * pairs:2].set(taker + passed)
    return lengths[jax.random.permutation(jax.random.fold_in(key, 2), amount)]


def gaussian(own_key, shape, scale, most, shards=(), held_as=jnp.bfloat16):
    values = jax.random.normal(own_key, shape, jnp.float32) * scale
    if len(shards) > 0:
        values = block_levels(own_key, shape, shards, -0.22, 0.18) * values
    return jnp.clip(values, min=-most, max=most).astype(held_as)


def setup_inputs(seed: int = 0) -> dict:
    key_list = jax.random.split(jax.random.key(seed), 16)
    block_input = gaussian(key_list[0], (TOKENS, D), 1.0, 6.0, ((0, 8),))
    seq_lengths = ragged_sizes(key_list[1], BATCH, BATCH * LEN // 2, LEN, 2).astype(jnp.int32)
    first_gain = jnp.clip(1.0 + 0.1 * jax.random.normal(key_list[2], (D,), jnp.float32), 0.5, 1.5)
    first_shift = gaussian(key_list[3], (D,), 0.5, 3.0, (), jnp.float32)
    qkv_weight = gaussian(key_list[4], (3, D, D), (D // 2) ** -0.5, 0.3125, ((2, 4),))
    qv_bias = gaussian(key_list[5], (2, D), 0.5, 3.0, ((1, 4),), jnp.float32)
    out_weight = gaussian(key_list[6], (D, D), 1 ** -0.5, 6.0, ((0, 4),))
    out_bias = gaussian(key_list[7], (D,), 1.0, 4.0, (), jnp.float32)
    second_gain = jnp.clip(1.0 + 0.1 * jax.random.normal(key_list[8], (D,), jnp.float32), 0.5, 1.5)
    second_shift = gaussian(key_list[9], (D,), 0.5, 3.0, (), jnp.float32)
    fc_weight = gaussian(key_list[10], (D, FF), D ** -0.5, 0.21875, ((1, 4),))
    fc_bias = gaussian(key_list[11], (FF,), 0.5, 3.0, ((0, 4),), jnp.float32)
    down_weight = gaussian(key_list[12], (FF, D), 24 ** -0.5, 1.25, ((0, 4),))
    down_bias = gaussian(key_list[13], (D,), 1.0, 4.0, (), jnp.float32)
    cotangent = gaussian(key_list[14], (TOKENS, D), 1.0, 6.0, ((0, 8),))
    return {"block_input": block_input, "seq_lengths": seq_lengths, "first_gain": first_gain, "first_shift": first_shift, "qkv_weight": qkv_weight, "qv_bias": qv_bias, "out_weight": out_weight, "out_bias": out_bias, "second_gain": second_gain, "second_shift": second_shift, "fc_weight": fc_weight, "fc_bias": fc_bias, "down_weight": down_weight, "down_bias": down_bias, "cotangent": cotangent}


branch_scale = 48.0 ** (-0.5)
norm_eps = 1e-05
masked_score = -1000000000.0
highest = lax.Precision.HIGHEST

@jax.custom_vjp
def low(v):
    return lax.optimization_barrier(v.astype(jnp.bfloat16)).astype(jnp.float32)

@jax.custom_vjp
def low_back(v):
    return v

def low_keep(v):
    return (low(v), None)

def low_pass(kept, grad):
    return (grad,)

def back_keep(v):
    return (v, None)

def back_low(kept, grad):
    return (low(grad),)
low.defvjp(low_keep, low_pass)
low_back.defvjp(back_keep, back_low)

def precise_dot(left, right):
    return jnp.dot(left, right, precision=highest, preferred_element_type=jnp.float32)

def layer_norm(values, gain, shift):
    row_mean = lax.optimization_barrier(jnp.mean(values, axis=-1, keepdims=True))
    centred = values - row_mean
    spread = lax.optimization_barrier(jnp.mean(centred * centred, axis=-1, keepdims=True))
    return centred * lax.rsqrt(spread + norm_eps) * gain + shift

def attend(operands):
    query_rows, key_rows, value_rows, length = operands
    seq_span = query_rows.shape[0]
    score_scale = query_rows.shape[2] ** (-0.5)
    raw = low_back(jnp.einsum('qhd,khd->hqk', query_rows, key_rows, precision=highest) * score_scale)
    row_index = lax.broadcasted_iota(jnp.int32, (seq_span, seq_span), 0)
    col_index = lax.broadcasted_iota(jnp.int32, (seq_span, seq_span), 1)
    allowed = (col_index <= row_index) & (col_index < length)
    scores = jnp.where(allowed[None], raw, masked_score)
    row_top = lax.optimization_barrier(jnp.max(scores, axis=-1, keepdims=True))
    weights = jnp.exp(scores - row_top)
    row_total = lax.optimization_barrier(jnp.sum(weights, axis=-1, keepdims=True))
    attn_probs = low(weights / row_total)
    mixed_rows = jnp.einsum('hqk,khd->qhd', attn_probs, value_rows, precision=highest)
    return low(low_back(mixed_rows))

def forward(block_in, first_gain, first_shift, qkv_weight, qv_bias, out_weight, out_bias, second_gain, second_shift, fc_weight, fc_bias, down_weight, down_bias, seq_lengths):
    tokens = block_in.shape[0]
    seq_count = seq_lengths.shape[0]
    seq_span = tokens // seq_count
    first_low = low(layer_norm(block_in, first_gain, first_shift))
    query_rows = low(low_back(precise_dot(first_low, qkv_weight[0]) + qv_bias[0]))
    key_rows = low(low_back(precise_dot(first_low, qkv_weight[1])))
    value_rows = low(low_back(precise_dot(first_low, qkv_weight[2]) + qv_bias[1]))
    shape_four = (seq_count, seq_span, HEADS, HD)
    mixed = lax.map(jax.checkpoint(attend), (query_rows.reshape(shape_four), key_rows.reshape(shape_four), value_rows.reshape(shape_four), seq_lengths))
    mixed = mixed.reshape(tokens, D)
    attention = low_back(precise_dot(mixed, out_weight)) + out_bias
    middle = block_in + branch_scale * attention
    second_low = low(layer_norm(middle, second_gain, second_shift))
    pre_act = low_back(precise_dot(second_low, fc_weight) + fc_bias)
    activ = low(jax.nn.gelu(pre_act, approximate=True))
    feed_sum = low_back(precise_dot(activ, down_weight)) + down_bias
    return middle + branch_scale * feed_sum

def reference(block_input, seq_lengths, first_gain, first_shift, qkv_weight, qv_bias, out_weight, out_bias, second_gain, second_shift, fc_weight, fc_bias, down_weight, down_bias, cotangent):
    floats = (block_input.astype(jnp.float32), first_gain.astype(jnp.float32), first_shift.astype(jnp.float32), qkv_weight.astype(jnp.float32), qv_bias.astype(jnp.float32), out_weight.astype(jnp.float32), out_bias.astype(jnp.float32), second_gain.astype(jnp.float32), second_shift.astype(jnp.float32), fc_weight.astype(jnp.float32), fc_bias.astype(jnp.float32), down_weight.astype(jnp.float32), down_bias.astype(jnp.float32))

    def apply_layer(*params):
        return forward(*params, seq_lengths)
    output, backward = jax.vjp(apply_layer, *floats)
    tokens = block_input.shape[0]
    seq_count = seq_lengths.shape[0]
    seq_span = tokens // seq_count
    places = lax.broadcasted_iota(jnp.int32, (seq_count, seq_span), 1)
    live_rows = jnp.where(places < seq_lengths[:, None], 1.0, 0.0).astype(jnp.float32).reshape(tokens, 1)
    grads = backward(cotangent.astype(jnp.float32) * live_rows)
    return (output.astype(jnp.bfloat16), grads[0], grads[1], grads[2], grads[3], grads[4], grads[5], grads[6], grads[7], grads[8], grads[9], grads[10], grads[11], grads[12])
```

```python
from functools import partial

import jax
import jax.numpy as jnp
from jax import lax
from jax.experimental import pallas as pl
from jax.experimental.pallas import tpu as pltpu
from jax.sharding import PartitionSpec as P

HD = 64
F32 = jnp.float32
BF16 = jnp.bfloat16

branch_scale = 48.0 ** (-0.5)
norm_eps = 1e-05
masked_score = -1000000000.0
gelu_a = 0.044715
gelu_c = (2.0 / 3.141592653589793) ** 0.5

TILE = 256
VMEM = pl.BlockSpec(memory_space=pltpu.VMEM)
SMEM = pl.BlockSpec(memory_space=pltpu.SMEM)

S_LEN, S_CORE, S_X, S_Y = 0, 1, 2, 3


def dot_nn(a, b):
    return jnp.dot(a, b, preferred_element_type=F32)


def dot_nt(a, b):
    return lax.dot_general(a, b, (((1,), (1,)), ((), ())), preferred_element_type=F32)


def dot_tn(a, b):
    return lax.dot_general(a, b, (((0,), (0,)), ((), ())), preferred_element_type=F32)


def unit_norm(v):
    mu = jnp.mean(v, axis=-1, keepdims=True)
    centred = v - mu
    spread = jnp.mean(centred * centred, axis=-1, keepdims=True)
    inv = lax.rsqrt(spread + norm_eps)
    return centred * inv, inv


def norm_back(q, u, inv, gain):
    w = q * gain
    m1 = jnp.mean(w, axis=-1, keepdims=True)
    m2 = jnp.mean(w * u, axis=-1, keepdims=True)
    return inv * (w - m1 - u * m2)


def rows_below(start, count, length):
    at = lax.broadcasted_iota(jnp.int32, (count, 1), 0) + start
    return at < length


def call(kernel, ins, outs, scratch=(), flops=0, nbytes=0, mib=40, trans=0, name=None):
    return pl.pallas_call(
        kernel,
        in_specs=[SMEM if a.dtype == jnp.int32 else VMEM for a in ins],
        out_specs=[VMEM for _ in outs],
        out_shape=[jax.ShapeDtypeStruct(s, d) for s, d in outs],
        scratch_shapes=list(scratch),
        compiler_params=pltpu.CompilerParams(vmem_limit_bytes=mib * 1024 * 1024),
        cost_estimate=pl.CostEstimate(flops=flops, bytes_accessed=nbytes, transcendentals=trans),
        name=name,
    )(*ins)


def fwd_kernel(sc, x_ref, g_ref, c_ref, w_ref, b_ref, low_ref, q_ref, k_ref, v_ref, mix_ref, pka_ref, pkb_ref, lse_ref):
    span, width = x_ref.shape
    cols = w_ref.shape[2]
    heads = cols // HD
    length = sc[S_LEN]
    tiles = span // TILE
    for i in range(tiles):
        rows = slice(i * TILE, (i + 1) * TILE)
        u, _ = unit_norm(x_ref[rows, :].astype(F32))
        low = (u * g_ref[...] + c_ref[...]).astype(BF16)
        low_ref[rows, :] = low
        q = (dot_nn(low, w_ref[0]) + b_ref[0:1, :]).astype(BF16)
        q_ref[rows, :] = q * BF16(HD**-0.5)
        k_ref[rows, :] = dot_nn(low, w_ref[1]).astype(BF16)
        v_ref[rows, :] = (dot_nn(low, w_ref[2]) + b_ref[1:2, :]).astype(BF16)
    key_bias = jnp.where(rows_below(0, span, length), 0.0, masked_score).astype(F32)
    causal = lax.broadcasted_iota(jnp.int32, (TILE, TILE), 0) <= lax.broadcasted_iota(jnp.int32, (TILE, TILE), 1)
    lse_ref[...] = jnp.zeros_like(lse_ref)
    for h in range(heads):
        hs = slice(h * HD, (h + 1) * HD)
        for t in range(tiles):
            rows = slice(t * TILE, (t + 1) * TILE)
            n = (t + 1) * TILE
            s = dot_nt(k_ref[0:n, hs], q_ref[rows, hs]) + key_bias[0:n]
            diag = jnp.where(causal, s[n - TILE :], masked_score)
            s = diag if t == 0 else jnp.concatenate([s[: n - TILE], diag], axis=0)
            top = jnp.max(s, axis=0, keepdims=True)
            e = jnp.exp(s - top)
            total = jnp.sum(e, axis=0, keepdims=True)
            p = (e * (1.0 / total)).astype(BF16)
            mix_ref[rows, hs] = dot_tn(p, v_ref[0:n, hs]).astype(BF16)
            lse_ref[h : h + 1, rows] = top + jnp.log(total)
    half = span // 2
    for part, ref in ((1, pka_ref), (0, pkb_ref)):
        base = part * half
        ref[0:half, :] = mix_ref[base : base + half, 0:128].astype(F32)
        lo = mix_ref[base : base + half // 2, 128:192].astype(F32)
        hi = mix_ref[base + half // 2 : base + half, 128:192].astype(F32)
        ref[half : half + half // 2, :] = jnp.concatenate([lo, hi], axis=1)


def weight_kernel(sc, own_ref, sib_ref, far_ref, fars_ref, out_ref):
    me = sc[S_X] * 2 + sc[S_CORE]
    for j, ref in enumerate((own_ref, sib_ref, far_ref, fars_ref)):
        w = ref[...].astype(BF16)
        at = me ^ j
        out_ref[pl.ds(pl.multiple_of(at * 128, 128), 128), :] = w[0:128]
        out_ref[pl.ds(pl.multiple_of(512 + at * 64, 64), 64), :] = w[128:192]


def ffn_kernel(
    part, sc, own_ref, sib_ref, far_ref, fars_ref, wo_ref, x_ref, cot_ref, ob_ref, g_ref, c_ref, fc_ref, fcb_ref, dn_ref,
    mid_ref, low_ref, act_ref, feed_ref, pg_ref, keep_ref, send_ref, buf,
):
    half, width = mid_ref.shape
    me = sc[S_X] * 2 + sc[S_CORE]
    core = sc[S_CORE]
    for j, ref in enumerate((own_ref, sib_ref, far_ref, fars_ref)):
        buf[:, pl.ds(pl.multiple_of((me ^ j) * 128, 128), 128)] = ref[0:half, :].astype(BF16)
    low_lanes = lax.broadcasted_iota(jnp.int32, (half // 2, 128), 1) < HD
    for j, (a_ref, b_ref) in enumerate(((own_ref, sib_ref), (far_ref, fars_ref))):
        a, b = a_ref[half:, :], b_ref[half:, :]
        first = jnp.where(core == 0, a, b)
        second = jnp.where(core == 0, b, a)
        at = pl.ds(pl.multiple_of(512 + (sc[S_X] ^ j) * 128, 128), 128)
        buf[0 : half // 2, at] = jnp.where(low_lanes, first, pltpu.roll(second, HD, 1)).astype(BF16)
        buf[half // 2 : half, at] = jnp.where(low_lanes, pltpu.roll(first, HD, 1), second).astype(BF16)
    base = part * half
    for t in range(half // TILE):
        rows = slice(t * TILE, (t + 1) * TILE)
        whole = slice(base + t * TILE, base + (t + 1) * TILE)
        attention = dot_nn(buf[rows, :], wo_ref[...]) + ob_ref[...]
        middle = x_ref[whole, :].astype(F32) + branch_scale * attention
        mid_ref[rows, :] = middle
        u, _ = unit_norm(middle)
        low = (u * g_ref[...] + c_ref[...]).astype(BF16)
        low_ref[rows, :] = low
        v = dot_nn(low, fc_ref[...]) + fcb_ref[...]
        v2 = v * v
        th = jnp.tanh(gelu_c * (v + gelu_a * (v2 * v)))
        half_up = 0.5 + 0.5 * th
        act_ref[rows, :] = (v * half_up).astype(BF16)
        slope = half_up + 0.5 * v * (1.0 - th * th) * (gelu_c + (3.0 * gelu_c * gelu_a) * v2)
        live = rows_below(base + t * TILE, TILE, sc[S_LEN])
        top = jnp.where(live, cot_ref[whole, :].astype(F32), 0.0)
        feed = (branch_scale * top).astype(BF16)
        feed_ref[rows, :] = feed
        pg = (dot_nt(feed, dn_ref[...]) * slope).astype(BF16)
        pg_ref[rows, :] = pg
        n2 = dot_nt(pg, fc_ref[...])

        @pl.when(core == t)
        def _():
            keep_ref[...] = n2

        @pl.when(core != t)
        def _():
            send_ref[...] = n2


def down_kernel(sc, acta_ref, actb_ref, feeda_ref, feedb_ref, dn_ref, keep_ref, send_ref, ka_ref, sa_ref, kb_ref, sb_ref):
    y, core = sc[S_Y], sc[S_CORE]
    rows = keep_ref.shape[0]
    for at, ref in ((y, keep_ref), (1 - y, send_ref)):
        cols = pl.ds(pl.multiple_of(at * rows, 128), rows)
        ref[...] = dot_tn(acta_ref[:, cols], feeda_ref[...]) + dot_tn(actb_ref[:, cols], feedb_ref[...])
    for act_ref, k_ref, s_ref in ((acta_ref, ka_ref, sa_ref), (actb_ref, kb_ref, sb_ref)):
        for at, ref in ((core, k_ref), (1 - core, s_ref)):
            ref[...] = dot_nn(act_ref[pl.ds(pl.multiple_of(at * TILE, TILE), TILE), :], dn_ref[...])


def fc_kernel(sc, lowa_ref, lowb_ref, pga_ref, pgb_ref, cot_ref, keep_ref, send_ref, small_ref):
    y = sc[S_Y]
    rows = keep_ref.shape[0]
    for at, ref in ((y, keep_ref), (1 - y, send_ref)):
        cols = pl.ds(pl.multiple_of(at * rows, 128), rows)
        ref[...] = dot_tn(lowa_ref[:, cols], pga_ref[...]) + dot_tn(lowb_ref[:, cols], pgb_ref[...])
    small_ref[...] = jnp.zeros_like(small_ref)
    total = jnp.zeros((1, pga_ref.shape[1]), F32)
    for ref in (pga_ref, pgb_ref):
        total = total + jnp.sum(ref[...].astype(F32), axis=0, keepdims=True)
    small_ref[0:1, :] = total
    total = jnp.zeros((1, cot_ref.shape[1]), F32)
    for t in range(cot_ref.shape[0] // TILE):
        live = rows_below(t * TILE, TILE, sc[S_LEN])
        top = jnp.where(live, cot_ref[t * TILE : (t + 1) * TILE, :].astype(F32), 0.0)
        total = total + jnp.sum(top * branch_scale, axis=0, keepdims=True)
    small_ref[1:2, :] = total


def attn_back_kernel(
    part, sc, own_ref, sib_ref, mid_ref, cot_ref, g_ref, wo_ref, q_ref, k_ref, v_ref, lse_ref, w_ref, *rest,
):
    if part == 1:
        mg_ref, ag_ref, dq_ref, dk_ref, dv_ref, small_ref, keep_ref, send_ref, ck_ref, cv_ref, ak, av = rest
        ik_ref = iv_ref = None
    else:
        ik_ref, iv_ref, mg_ref, ag_ref, dq_ref, dk_ref, dv_ref, small_ref, keep_ref, send_ref, ak, av = rest
    half, width = mid_ref.shape
    cols = q_ref.shape[1]
    heads = cols // HD
    core, length = sc[S_CORE], sc[S_LEN]
    base = part * half
    tiles = half // TILE
    span_keys = base + half
    small_ref[...] = jnp.zeros_like(small_ref)
    if part == 1:
        ak[...] = jnp.zeros_like(ak)
        av[...] = jnp.zeros_like(av)
    else:
        ak[...] = ik_ref[...]
        av[...] = iv_ref[...]
    key_bias = jnp.where(rows_below(0, span_keys, length), 0.0, masked_score).astype(F32)
    causal = lax.broadcasted_iota(jnp.int32, (TILE, TILE), 0) <= lax.broadcasted_iota(jnp.int32, (TILE, TILE), 1)
    for t in range(tiles):
        rows = slice(t * TILE, (t + 1) * TILE)
        whole = slice(base + t * TILE, base + (t + 1) * TILE)
        q2 = jnp.where(core == t, own_ref[...], sib_ref[...])
        u, inv = unit_norm(mid_ref[rows, :])
        live = rows_below(base + t * TILE, TILE, length)
        top = jnp.where(live, cot_ref[whole, :].astype(F32), 0.0)
        mg = top + norm_back(q2, u, inv, g_ref[...])
        mg_ref[rows, :] = mg
        small_ref[0:1, :] += jnp.sum(q2 * u, axis=0, keepdims=True)
        small_ref[1:2, :] += jnp.sum(q2, axis=0, keepdims=True)
        branch = branch_scale * mg
        small_ref[2:3, :] += jnp.sum(branch, axis=0, keepdims=True)
        ag = branch.astype(BF16)
        ag_ref[rows, :] = ag
        mixed_grad = dot_nt(ag, wo_ref[...]).astype(BF16)
        n = base + (t + 1) * TILE
        for h in range(heads):
            hs = slice(h * HD, (h + 1) * HD)
            q = q_ref[whole, hs]
            do = mixed_grad[:, hs]
            k = k_ref[0:n, hs]
            s = dot_nt(k, q) + key_bias[0:n]
            diag = jnp.where(causal, s[n - TILE :], masked_score)
            s = diag if n == TILE else jnp.concatenate([s[: n - TILE], diag], axis=0)
            p = jnp.exp(s - lse_ref[h : h + 1, whole])
            dp = dot_nt(v_ref[0:n, hs], do)
            inner = jnp.sum(p * dp, axis=0, keepdims=True)
            ds = (p * (dp - inner)).astype(BF16)
            av[0:n, hs] += dot_nn(p.astype(BF16), do)
            ak[0:n, hs] += dot_nn(ds, q)
            dq_ref[rows, hs] = (dot_tn(ds, k) * (HD**-0.5)).astype(BF16)
    dk_ref[...] = ak[base:span_keys, :].astype(BF16)
    dv_ref[...] = av[base:span_keys, :].astype(BF16)
    if part == 1:
        ck_ref[...] = ak[0:base, :]
        cv_ref[...] = av[0:base, :]
    for t in range(tiles):
        rows = slice(t * TILE, (t + 1) * TILE)
        n1 = dot_nt(dq_ref[rows, :], w_ref[0]) + dot_nt(dk_ref[rows, :], w_ref[1]) + dot_nt(dv_ref[rows, :], w_ref[2])

        @pl.when(core == t)
        def _():
            keep_ref[...] = n1

        @pl.when(core != t)
        def _():
            send_ref[...] = n1


def qkv_grad_kernel(
    sc, low_ref, mix_ref, aga_ref, agb_ref, dqa_ref, dqb_ref, dka_ref, dkb_ref, dva_ref, dvb_ref,
    keep_ref, send_ref, small_ref,
):
    y = sc[S_Y]
    half = aga_ref.shape[0]
    cols = mix_ref.shape[1]
    lowa, lowb = low_ref.at[half:, :], low_ref.at[:half, :]
    blocks = (
        ((dqa_ref, lowa), (dqb_ref, lowb)),
        ((dka_ref, lowa), (dkb_ref, lowb)),
        ((dva_ref, lowa), (dvb_ref, lowb)),
        ((mix_ref.at[half:, :], aga_ref), (mix_ref.at[:half, :], agb_ref)),
    )
    for i, pairs in enumerate(blocks):
        total = sum(dot_tn(a[...], b[...]) for a, b in pairs)
        rows = slice((i % 2) * cols, (i % 2 + 1) * cols)

        @pl.when(y == i // 2)
        def _():
            keep_ref[rows, :] = total

        @pl.when(y != i // 2)
        def _():
            send_ref[rows, :] = total

    small_ref[...] = jnp.zeros_like(small_ref)
    for i, (a_ref, b_ref) in enumerate(((dqa_ref, dqb_ref), (dva_ref, dvb_ref))):
        small_ref[i : i + 1, :] = jnp.sum(a_ref[...].astype(F32), axis=0, keepdims=True) + jnp.sum(
            b_ref[...].astype(F32), axis=0, keepdims=True
        )


def input_kernel(sc, x_ref, g_ref, owna_ref, siba_ref, ownb_ref, sibb_ref, mga_ref, mgb_ref, out_ref, small_ref):
    core = sc[S_CORE]
    small_ref[...] = jnp.zeros_like(small_ref)
    half = mga_ref.shape[0]
    for part, own_ref, sib_ref, mg_ref in ((0, ownb_ref, sibb_ref, mgb_ref), (1, owna_ref, siba_ref, mga_ref)):
        for t in range(half // TILE):
            rows = slice(t * TILE, (t + 1) * TILE)
            whole = slice(part * half + t * TILE, part * half + (t + 1) * TILE)
            q1 = jnp.where(core == t, own_ref[...], sib_ref[...])
            u, inv = unit_norm(x_ref[whole, :].astype(F32))
            out_ref[whole, :] = mg_ref[rows, :] + norm_back(q1, u, inv, g_ref[...])
            small_ref[0:1, :] += jnp.sum(q1 * u, axis=0, keepdims=True)
            small_ref[1:2, :] += jnp.sum(q1, axis=0, keepdims=True)


def output_kernel(sc, b_ref, owna_ref, siba_ref, ownb_ref, sibb_ref, mida_ref, midb_ref, out_ref):
    core = sc[S_CORE]
    half = mida_ref.shape[0]
    for part, own_ref, sib_ref, mid_ref in ((0, ownb_ref, sibb_ref, midb_ref), (1, owna_ref, siba_ref, mida_ref)):
        for t in range(half // TILE):
            rows = slice(t * TILE, (t + 1) * TILE)
            whole = slice(part * half + t * TILE, part * half + (t + 1) * TILE)
            total = jnp.where(core == t, own_ref[...], sib_ref[...])
            out_ref[whole, :] = (mid_ref[rows, :] + branch_scale * (total + b_ref[...])).astype(BF16)


def swap(v, axis, size, bit):
    return lax.ppermute(v, axis, [(i, i ^ bit) for i in range(size)])


def sum_rest(keep, send, mp):
    own = keep + swap(send, "mp", mp, 1)
    own = own + swap(own, "mp", mp, 2)
    return own, swap(own, "mp", mp, 1)


def split(v, bit):
    half = v.shape[0] // 2
    first, second = v[:half], v[half:]
    return jnp.where(bit == 0, first, second), jnp.where(bit == 0, second, first)


def join(mine, other, bit):
    return jnp.where(bit == 0, jnp.concatenate([mine, other]), jnp.concatenate([other, mine]))


def sum_dp(keep, send, dp, index):
    if dp != 8:
        return lax.psum(jnp.concatenate([keep, send]), "dp")
    y, z0, z1 = index % 2, (index // 2) % 2, index // 4
    keep = keep + swap(send, "dp", dp, 1)
    keep, send = split(keep, z0)
    keep = keep + swap(send, "dp", dp, 2)
    keep, send = split(keep, z1)
    keep = keep + swap(send, "dp", dp, 4)
    keep = join(keep, swap(keep, "dp", dp, 4), z1)
    keep = join(keep, swap(keep, "dp", dp, 2), z0)
    return join(keep, swap(keep, "dp", dp, 1), y)


def sum_small(v, dp):
    if dp != 8:
        return lax.psum(v, "dp")
    for bit in (1, 2, 4):
        v = v + swap(v, "dp", dp, bit)
    return v


def shards(
    dp,
    mp,
    block_input,
    seq_lengths,
    first_gain,
    first_shift,
    qkv_weight,
    qv_bias,
    out_weight,
    out_bias,
    second_gain,
    second_shift,
    fc_weight,
    fc_bias,
    down_weight,
    down_bias,
    cotangent,
):
    span, width = block_input.shape
    half = span // 2
    cols = qkv_weight.shape[2]
    hidden = fc_weight.shape[1]
    at_mp, at_dp = lax.axis_index("mp"), lax.axis_index("dp")
    y_bit = at_dp % 2 if dp == 8 else jnp.int32(0)
    sc = jnp.stack([seq_lengths[0], at_mp % 2, at_mp // 2, y_bit]).astype(jnp.int32)
    row = lambda v: v.reshape(1, -1)
    mm = lambda *d: 2 * d[0] * d[1] * d[2]

    w_own = out_weight.astype(F32)
    w_sib = swap(w_own, "mp", mp, 1)
    w_far = swap(w_own, "mp", mp, 2)
    w_fars = swap(w_far, "mp", mp, 1)

    low, q, k, v, mix, pka, pkb, lse = call(
        fwd_kernel,
        (sc, block_input, row(first_gain), row(first_shift), qkv_weight, qv_bias),
        (
            ((span, width), BF16),
            ((span, cols), BF16),
            ((span, cols), BF16),
            ((span, cols), BF16),
            ((span, cols), BF16),
            ((half * 3 // 2, 128), F32),
            ((half * 3 // 2, 128), F32),
            ((8, span), F32),
        ),
        flops=mm(span, width, 3 * cols) * 4,
        nbytes=8 << 20,
        name="attn",
    )
    (wo_all,) = call(
        weight_kernel, (sc, w_own, w_sib, w_far, w_fars), (((width, width), BF16),), nbytes=4 << 20, name="wo"
    )

    def gather(own):
        sib = swap(own, "mp", mp, 1)
        far = swap(own, "mp", mp, 2)
        return own, sib, far, swap(far, "mp", mp, 1)

    def ffn(part, pieces):
        return call(
            partial(ffn_kernel, part),
            (
                sc, *pieces, wo_all, block_input, cotangent, row(out_bias), row(second_gain), row(second_shift),
                fc_weight, row(fc_bias), down_weight,
            ),
            (
                ((half, width), F32),
                ((half, width), BF16),
                ((half, hidden), BF16),
                ((half, width), BF16),
                ((half, hidden), BF16),
                ((half // 2, width), F32),
                ((half // 2, width), F32),
            ),
            scratch=[pltpu.VMEM((half, width), BF16)],
            flops=mm(half, width, hidden) * 8,
            nbytes=16 << 20,
            name=f"ffn{part}",
        )

    pieces_a = gather(pka)
    pieces_b = gather(pkb)
    mid_a, low_a, act_a, feed_a, pg_a, n2k_a, n2s_a = ffn(1, pieces_a)
    n2_a = sum_rest(n2k_a, n2s_a, mp)
    mid_b, low_b, act_b, feed_b, pg_b, n2k_b, n2s_b = ffn(0, pieces_b)
    n2_b = sum_rest(n2k_b, n2s_b, mp)

    dgk, dgs, oka, osa, okb, osb = call(
        down_kernel,
        (sc, act_a, act_b, feed_a, feed_b, down_weight),
        (
            ((hidden // 2, width), F32),
            ((hidden // 2, width), F32),
            ((half // 2, width), F32),
            ((half // 2, width), F32),
            ((half // 2, width), F32),
            ((half // 2, width), F32),
        ),
        flops=mm(span, width, hidden) * 4,
        nbytes=14 << 20,
        name="down",
    )
    fgk, fgs, small_f = call(
        fc_kernel,
        (sc, low_a, low_b, pg_a, pg_b, cotangent),
        (((width // 2, hidden), F32), ((width // 2, hidden), F32), ((8, width), F32)),
        flops=mm(span, width, hidden) * 3,
        nbytes=8 << 20,
        name="fc",
    )
    down_weight_grad = sum_dp(dgk, dgs, dp, at_dp)
    fc_weight_grad = sum_dp(fgk, fgs, dp, at_dp)

    def attn_back(part, total, mid, carry):
        keys = (part + 1) * half
        outs = [
            ((half, width), F32),
            ((half, width), BF16),
            ((half, cols), BF16),
            ((half, cols), BF16),
            ((half, cols), BF16),
            ((8, width), F32),
            ((half // 2, width), F32),
            ((half // 2, width), F32),
        ]
        if part == 1:
            outs += [((half, cols), F32), ((half, cols), F32)]
        return call(
            partial(attn_back_kernel, part),
            (sc, *total, mid, cotangent, row(second_gain), out_weight, q, k, v, lse, qkv_weight, *carry),
            outs,
            scratch=[pltpu.VMEM((keys, cols), F32), pltpu.VMEM((keys, cols), F32)],
            flops=mm(half, width, cols) * 16,
            nbytes=16 << 20,
            name=f"back{part}",
        )

    mg_a, ag_a, dq_a, dk_a, dv_a, small_a, n1k_a, n1s_a, ck, cv = attn_back(1, n2_a, mid_a, ())
    n1_a = sum_rest(n1k_a, n1s_a, mp)
    mg_b, ag_b, dq_b, dk_b, dv_b, small_b, n1k_b, n1s_b = attn_back(0, n2_b, mid_b, (ck, cv))
    n1_b = sum_rest(n1k_b, n1s_b, mp)

    qgk, qgs, small_q = call(
        qkv_grad_kernel,
        (sc, low, mix, ag_a, ag_b, dq_a, dq_b, dk_a, dk_b, dv_a, dv_b),
        (((2 * cols, width), F32), ((2 * cols, width), F32), ((8, cols), F32)),
        flops=mm(span, width, cols) * 6,
        nbytes=10 << 20,
        name="qkvg",
    )
    proj_grad = sum_dp(qgk, qgs, dp, at_dp)

    out_a = sum_rest(oka, osa, mp)
    out_b = sum_rest(okb, osb, mp)

    input_grad, small_i = call(
        input_kernel,
        (sc, block_input, row(first_gain), *n1_a, *n1_b, mg_a, mg_b),
        (((span, width), F32), ((8, width), F32)),
        nbytes=12 << 20,
        name="ingrad",
    )
    (block_output,) = call(
        output_kernel,
        (sc, row(down_bias), *out_a, *out_b, mid_a, mid_b),
        (((span, width), BF16),),
        nbytes=10 << 20,
        name="out",
    )

    qv_small = jnp.pad(small_q[0:2], ((0, 0), (0, width - cols)))
    smalls = jnp.concatenate([small_f[0:2], small_a[0:3] + small_b[0:3], small_i[0:2], qv_small])
    smalls = sum_small(jnp.pad(smalls, ((0, 16 - smalls.shape[0]), (0, 0))), dp)

    qkv_grad = jnp.stack([proj_grad[i * cols : (i + 1) * cols].T for i in range(3)])
    out_weight_grad = proj_grad[3 * cols :]
    return (
        block_output,
        input_grad,
        smalls[5],
        smalls[6],
        qkv_grad,
        smalls[7:9, :cols],
        out_weight_grad,
        smalls[4],
        smalls[2],
        smalls[3],
        fc_weight_grad,
        smalls[0],
        down_weight_grad,
        smalls[1],
    )


def solution(mesh):
    in_specs = (
        P("dp", None),
        P("dp"),
        P(),
        P(),
        P(None, None, "mp"),
        P(None, "mp"),
        P("mp", None),
        P(),
        P(),
        P(),
        P(None, "mp"),
        P("mp"),
        P("mp", None),
        P(),
        P("dp", None),
    )
    out_specs = (
        P("dp", None),
        P("dp", None),
        P(),
        P(),
        P(None, None, "mp"),
        P(None, "mp"),
        P("mp", None),
        P(),
        P(),
        P(),
        P(None, "mp"),
        P("mp"),
        P("mp", None),
        P(),
    )
    body = partial(shards, mesh.shape["dp"], mesh.shape["mp"])
    return jax.shard_map(body, mesh=mesh, in_specs=in_specs, out_specs=out_specs, check_vma=False)
```
